128 devices in a mesh: slot: 16 (over y, z), shard: 8 (over x, core).
Axes of the slice: x: 4, y: 4, z: 4, core: 2. Of those that a mesh axis runs over, the one named last changes fastest.
Arguments:
- acts: bfloat16 [16, 3072, 1024], P('slot'), may hold values from -6 to 6
- out_grads: bfloat16 [16, 3072, 7168], P('slot', None, 'shard'), may hold values from -6 to 6
- counts: int32 [16], P('slot'), may hold values from 128 to 3072, as said below
- replica_map: int32 [16], replicated, may hold values from 0 to 3, as said below
- next_map: int32 [16], replicated, may hold values from 0 to 3, as said below
- slot_weights: bfloat16 [16, 1024, 7168], P('slot', None, 'shard'), may hold values from -6 to 6
- master: float32 [4096, 7168], P('slot', 'shard'), may hold values from -6 to 6
- moment1: float32 [4096, 7168], P('slot', 'shard'), may hold values from -1.75 to 1.75
- moment2: float32 [4096, 7168], P('slot', 'shard'), may hold values from 0.05 to 2
Outputs:
- new_weights: bfloat16 [16, 1024, 7168], P('slot', None, 'shard')
- new_master: float32 [4096, 7168], P('slot', 'shard')
- new_moment1: float32 [4096, 7168], P('slot', 'shard')
- new_moment2: float32 [4096, 7168], P('slot', 'shard')
- act_grads: bfloat16 [16, 3072, 1024], P('slot', None, 'shard')
The draws below stay inside these ranges and needn't reach their ends.
Inputs may be any that keep to these rules, and one draw needn't show every extreme that they name: `counts`: every entry is a multiple of 128; some slot has exactly 3072 and some exactly 128. `replica_map`: every expert is held by at least 2 slots and at most 8; one expert by exactly 8. `next_map`: every expert is held by at least 2 slots and at most 8; one expert by exactly 8.
All inputs are finite; a program needn't handle non-finite values.
Results may differ from the reference program's by a relative error of at most 0.017.
Values may be sent and summed in bfloat16 or wider, within the bound.
No kernel may reach another device: no remote copies, remote signals or barrier semaphores. Data moves between devices by JAX's collectives and lax.ppermute only.
A program may use at most 128 MiB of HBM per device.

```python
import math
import jax
import jax.numpy as jnp
from jax import lax

D = 7168
FF = 1024
TOK = 3072
SLOTS = 16
EXPERTS = 4
ROWS = 4096
D_SH = 896
MAX_REP = 8
N_SHARD = 8


def place_experts(key):
    key_busy, key_offset, key_order = jax.random.split(key, 3)
    busiest = jax.random.randint(key_busy, (), 0, EXPERTS)
    others = (busiest + 1 + jnp.arange(EXPERTS - 1)) % EXPERTS
    extra_slots = SLOTS - MAX_REP - 2 * (EXPERTS - 1)
    offset = jax.random.randint(key_offset, (), 0, max(EXPERTS - 1, 1))
    spare_slots = others[(offset + jnp.arange(extra_slots)) % max(EXPERTS - 1, 1)]
    listed = jnp.concatenate([jnp.full((MAX_REP,), busiest), jnp.repeat(others, 2), spare_slots]).astype(jnp.int32)
    return jax.random.permutation(key_order, listed).astype(jnp.int32)


def draw_replica_map(key, part):
    key = jax.random.fold_in(key, 11)
    return place_experts(key)


def draw_next_map(key, part):
    key = jax.random.fold_in(key, 12)
    return place_experts(key)


def draw_counts(key, part):
    key = jax.random.fold_in(key, 13)
    key_draw, key_pick = jax.random.split(key)
    block_total = TOK // 128
    raw_draw = jax.random.randint(key_draw, (SLOTS,), 0, block_total)
    blocks = 1 + raw_draw * raw_draw // block_total
    chosen = jax.random.permutation(key_pick, SLOTS)
    blocks = blocks.at[chosen[0]].set(block_total).at[chosen[1]].set(1)
    return (blocks * 128).astype(jnp.int32)


def steps_of(key, extent, shards, smallest, largest):
    gain = 1.0
    for position, shards_of in shards:
        heights = jax.random.uniform(jax.random.fold_in(jax.random.fold_in(key, 6), position), (shards_of,), jnp.float32, smallest / len(shards), largest / len(shards))
        gain = gain * jnp.repeat(jnp.exp(heights), extent[position] // shards_of).reshape((-1,) + (1,) * (len(extent) - 1 - position))
    return gain


def scatter_about(rng, shape, scale, most, pieces=(), kind=jnp.bfloat16):
    drawn = jax.random.normal(rng, shape, jnp.float32) * scale
    if len(pieces) > 0:
        drawn = steps_of(rng, shape, pieces, -0.22, 0.18) * drawn
    return jnp.clip(drawn, min=-most, max=most).astype(kind)


def setup_inputs(seed: int = 0) -> dict:
    streams_of = jax.random.split(jax.random.key(seed), 10)
    acts = scatter_about(streams_of[0], (SLOTS, TOK, FF), 1.0, 6.0, ((0, 16),))
    out_grads = scatter_about(streams_of[1], (SLOTS, TOK, D), 1.0, 6.0, ((0, 16), (2, 8)))
    counts = draw_counts(jax.random.fold_in(streams_of[9], 71), 0)
    replica_map = draw_replica_map(jax.random.fold_in(streams_of[9], 71), 0)
    next_map = draw_next_map(jax.random.fold_in(streams_of[9], 71), 0)
    slot_weights = scatter_about(streams_of[5], (SLOTS, FF, D), 1.0, 6.0, ((0, 16), (2, 8)))
    master = scatter_about(streams_of[6], (ROWS, D), 1.0, 6.0, ((0, 16), (1, 8)), jnp.float32)
    moment1 = scatter_about(streams_of[7], (ROWS, D), 0.3, 1.75, ((0, 16), (1, 8)), jnp.float32)
    moment2 = jnp.clip(jnp.exp(math.log(2.0) - 3.6888794 * jax.random.uniform(streams_of[8], (ROWS, D), jnp.float32) ** steps_of(streams_of[8], (ROWS, D), ((0, 16), (1, 8)), -0.2, 0.2)), 0.05, 2.0)
    return {"acts": acts, "out_grads": out_grads, "counts": counts, "replica_map": replica_map, "next_map": next_map, "slot_weights": slot_weights, "master": master, "moment1": moment1, "moment2": moment2}


beta_one = 0.9
beta_two = 0.95
learn_rate = 0.5
weight_decay = 0.1
epsilon = 1e-08
adam_step = 20

def adam_update(grad_total, master, moment1, moment2):
    new_first = beta_one * moment1 + (1.0 - beta_one) * grad_total
    new_second = beta_two * moment2 + (1.0 - beta_two) * grad_total * grad_total
    first_hat = new_first / (1.0 - beta_one ** adam_step)
    second_hat = new_second / (1.0 - beta_two ** adam_step)
    update = first_hat / (jnp.sqrt(second_hat) + epsilon)
    master_new = master - learn_rate * (update + weight_decay * master)
    return (master_new, new_first, new_second)

def reference(acts, out_grads, counts, replica_map, next_map, slot_weights, master, moment1, moment2):
    unit_scale = FF ** (-0.5)
    positions = jnp.arange(TOK, dtype=jnp.int32)

    def per_slot(grad_total, slot_items):
        hidden, grad_out, count_here, expert_here, weight = slot_items
        masked = jnp.where((positions < count_here)[:, None], grad_out, jnp.zeros_like(grad_out))
        slot_grad = (jnp.dot(hidden.T, masked, preferred_element_type=jnp.float32) * unit_scale).astype(jnp.bfloat16)
        slot_grad = lax.optimization_barrier(slot_grad)
        row_start = (expert_here * FF).astype(jnp.int32)
        expert_rows = lax.dynamic_slice_in_dim(grad_total, row_start, FF, 0)
        grad_total = lax.dynamic_update_slice_in_dim(grad_total, expert_rows + slot_grad.astype(jnp.float32), row_start, 0)
        summed = jnp.zeros((TOK, FF), jnp.float32)
        for block_index in range(N_SHARD):
            lower = block_index * D_SH
            shard_term = jnp.dot(masked[:, lower:lower + D_SH], weight[:, lower:lower + D_SH].T, preferred_element_type=jnp.float32) * unit_scale
            rounded_term = lax.optimization_barrier(shard_term.astype(jnp.bfloat16))
            summed = summed + rounded_term.astype(jnp.float32)
        return (grad_total, summed.astype(jnp.bfloat16))
    grad_total, act_grads = lax.scan(per_slot, jnp.zeros((ROWS, D), jnp.float32), (acts, out_grads, counts, replica_map, slot_weights))
    master_new, new_first, new_second = adam_update(grad_total, master, moment1, moment2)
    new_weights = master_new.reshape(EXPERTS, FF, D)[next_map].astype(jnp.bfloat16)
    return (new_weights, master_new, new_first, new_second, act_grads)
```

```python
import functools

import jax
import jax.numpy as jnp
from jax import lax
from jax.experimental import pallas as pl
from jax.experimental.pallas import tpu as pltpu
from jax.sharding import PartitionSpec as P

beta_one = 0.9
beta_two = 0.95
learn_rate = 0.5
weight_decay = 0.1
epsilon = 1e-08
adam_step = 20

RING = 4
CHUNKS = 2
bf16 = jnp.bfloat16
f32 = jnp.float32


def params(*semantics):
    return pltpu.CompilerParams(vmem_limit_bytes=56 << 20, dimension_semantics=semantics or None)


def shift_z(value, step):
    return lax.ppermute(value, "slot", [(RING * y + z, RING * y + (z + step) % RING) for y in range(RING) for z in range(RING)])


def shift_y(value, step):
    return lax.ppermute(value, "slot", [(RING * y + z, RING * ((y + step) % RING) + z) for y in range(RING) for z in range(RING)])


def shift_x(value, step):
    return lax.ppermute(value, "shard", [(2 * x + c, 2 * ((x + step) % RING) + c) for x in range(RING) for c in range(2)])


def swap_core(value):
    return lax.ppermute(value, "shard", [(i, i ^ 1) for i in range(2 * RING)])


def exchange(shift, pieces):
    ahead, behind, across = shift(pieces[1], 1), shift(pieces[3], -1), shift(pieces[2], 2)
    return [pieces[0], behind, across, ahead]


def slot_grads(counts, acts, out_grads, scale):
    tokens, ff = acts.shape
    width = out_grads.shape[1]
    block = 1024
    steps = tokens // block
    quarter = ff // RING
    part = quarter // CHUNKS

    def kernel(count_ref, acts_ref, grads_ref, *rest):
        outs, total = rest[:-1], rest[-1]
        step = pl.program_id(0)
        here = lax.axis_index("slot") % RING
        live = count_ref[0] - step * block
        rows = lax.broadcasted_iota(jnp.int32, (block, width), 0)
        grads = grads_ref[...]
        masked = jnp.where(rows < live, grads, jnp.zeros_like(grads))
        term = lax.dot_general(masked, acts_ref[...], (((0,), (0,)), ((), ())), preferred_element_type=f32)

        @pl.when(step == 0)
        def _():
            total[...] = term

        @pl.when(step > 0)
        def _():
            total[...] += term

        @pl.when(step == steps - 1)
        def _():
            for chunk in range(CHUNKS):
                for distance in range(RING):
                    start = ((here + distance) % RING) * quarter + chunk * part
                    columns = total[:, pl.ds(pl.multiple_of(start, part), part)]
                    outs[chunk * RING + distance][...] = (columns * scale).astype(bf16)

    pieces = pl.pallas_call(
        kernel,
        grid_spec=pltpu.PrefetchScalarGridSpec(
            num_scalar_prefetch=1,
            grid=(steps,),
            in_specs=[
                pl.BlockSpec((block, ff), lambda i, c: (i, 0)),
                pl.BlockSpec((block, width), lambda i, c: (i, 0)),
            ],
            out_specs=[pl.BlockSpec((width, part), lambda i, c: (0, 0))] * (CHUNKS * RING),
            scratch_shapes=[pltpu.VMEM((width, ff), f32)],
        ),
        out_shape=[jax.ShapeDtypeStruct((width, part), bf16)] * (CHUNKS * RING),
        compiler_params=params("arbitrary"),
        cost_estimate=pl.CostEstimate(flops=2 * tokens * ff * width, bytes_accessed=14_000_000, transcendentals=0),
        name="slot_grads",
    )(counts, acts, out_grads)
    return [pieces[chunk * RING : (chunk + 1) * RING] for chunk in range(CHUNKS)]


def act_terms(place, half, halves, out_grads, other_grads, weight, other_weight, scale):
    tokens, width = out_grads.shape
    ff = weight.shape[0]
    block = 512
    here_tokens = tokens // halves
    steps = here_tokens // block
    columns = ff // (2 * RING)
    first = half * steps

    def kernel(place_ref, grads_ref, other_ref, *rest):
        weights, outs = rest[: 2 * RING], rest[2 * RING :]
        live = place_ref[2] - (first + pl.program_id(0)) * block
        both = jnp.concatenate([grads_ref[...], other_ref[...]], axis=1)
        own = jnp.concatenate([w[...].reshape(columns, width) for w in weights[:RING]], axis=0)
        other = jnp.concatenate([w[...].reshape(columns, width) for w in weights[RING:]], axis=0)
        matrix = jnp.concatenate([own, other], axis=1)
        term = lax.dot_general(both, matrix, (((1,), (1,)), ((), ())), preferred_element_type=f32) * scale
        rows = lax.broadcasted_iota(jnp.int32, term.shape, 0)
        term = jnp.where(rows < live, term, 0.0).astype(bf16)
        for distance in range(RING):
            outs[distance][...] = term[:, distance * columns : (distance + 1) * columns]

    def rows_of(distance):
        return pl.BlockSpec((1, 1, columns, width), lambda i, p: ((p[0] + distance) % RING, p[1], 0, 0))

    split = (RING, 2, columns, width)
    return pl.pallas_call(
        kernel,
        grid_spec=pltpu.PrefetchScalarGridSpec(
            num_scalar_prefetch=1,
            grid=(steps,),
            in_specs=[pl.BlockSpec((block, width), lambda i, p: (first + i, 0))] * 2
            + [rows_of(distance) for distance in range(RING)] * 2,
            out_specs=[pl.BlockSpec((block, columns), lambda i, p: (i, 0))] * RING,
        ),
        out_shape=[jax.ShapeDtypeStruct((here_tokens, columns), bf16)] * RING,
        compiler_params=params("arbitrary"),
        cost_estimate=pl.CostEstimate(flops=2 * here_tokens * ff * width, bytes_accessed=9_000_000, transcendentals=0),
        name="act_terms",
    )(place, out_grads, other_grads, *([weight.reshape(split)] * RING), *([other_weight.reshape(split)] * RING))


def act_sum(halves):
    rows, columns = halves[0][0].shape
    count = len(halves)

    def kernel(*refs):
        ins, out = refs[:-1], refs[-1]
        for half in range(count):

            @pl.when(pl.program_id(0) == half)
            def _(half=half):
                terms = [ref[...].astype(f32) for ref in ins[half * RING : (half + 1) * RING]]
                out[...] = ((terms[0] + terms[1]) + (terms[2] + terms[3])).astype(bf16)

    return pl.pallas_call(
        kernel,
        grid=(count,),
        in_specs=[pl.BlockSpec((rows, columns), lambda i: (0, 0))] * (count * RING),
        out_specs=pl.BlockSpec((rows, columns), lambda i: (i, 0)),
        out_shape=jax.ShapeDtypeStruct((count * rows, columns), bf16),
        compiler_params=params("arbitrary"),
        cost_estimate=pl.CostEstimate(flops=4 * count * rows * columns, bytes_accessed=8_000_000, transcendentals=0),
        name="act_sum",
    )(*[piece for half in halves for piece in half])


def by_expert(replica_map, pieces):
    def kernel(map_ref, *refs):
        ins, outs = refs[:RING], refs[RING:]
        slot = lax.axis_index("slot")
        y, z = slot // RING, slot % RING
        values = [ref[...].astype(f32) for ref in ins]
        held = [map_ref[RING * y + (z + distance) % RING] for distance in range(RING)]
        for step in range(RING):
            expert = (y + step) % RING
            total = jnp.where(held[0] == expert, values[0], 0.0)
            for value, one in zip(values[1:], held[1:]):
                total = total + jnp.where(one == expert, value, 0.0)
            outs[step][...] = total.astype(bf16)

    shape = pieces[0].shape
    return pl.pallas_call(
        kernel,
        grid_spec=pltpu.PrefetchScalarGridSpec(
            num_scalar_prefetch=1,
            grid=(1,),
            in_specs=[pl.BlockSpec(shape, lambda i, m: (0, 0))] * RING,
            out_specs=[pl.BlockSpec(shape, lambda i, m: (0, 0))] * RING,
        ),
        out_shape=[jax.ShapeDtypeStruct(shape, bf16)] * RING,
        compiler_params=params("arbitrary"),
        cost_estimate=pl.CostEstimate(flops=1_000_000, bytes_accessed=2_000_000, transcendentals=0),
        name="by_expert",
    )(replica_map, *pieces)


def adam_update(grad_total, master, moment1, moment2):
    new_first = beta_one * moment1 + (1.0 - beta_one) * grad_total
    new_second = beta_two * moment2 + (1.0 - beta_two) * grad_total * grad_total
    first_hat = new_first / (1.0 - beta_one**adam_step)
    second_hat = new_second / (1.0 - beta_two**adam_step)
    update = first_hat / (jnp.sqrt(second_hat) + epsilon)
    master_new = master - learn_rate * (update + weight_decay * master)
    return (master_new, new_first, new_second)


def adam(chunk, pieces, state, earlier):
    rows, width = state[0].shape
    part = rows // CHUNKS

    def kernel(*refs):
        terms = [ref[...].astype(f32) for ref in refs[:RING]]
        master, moment1, moment2 = refs[RING : RING + 3]
        outs = refs[-4:]
        grad = ((terms[0] + terms[1]) + (terms[2] + terms[3])).T
        master_new, new_first, new_second = adam_update(grad, master[...], moment1[...], moment2[...])
        outs[0][...] = master_new
        outs[1][...] = new_first
        outs[2][...] = new_second
        outs[3][...] = master_new.astype(bf16)

    whole = jax.ShapeDtypeStruct((rows, width), f32)
    mine = pl.BlockSpec((part, width), lambda i: (chunk, 0))
    return pl.pallas_call(
        kernel,
        grid=(1,),
        in_specs=[pl.BlockSpec((width, part), lambda i: (0, 0))] * RING
        + [mine] * 3
        + [pl.BlockSpec(memory_space=pl.ANY)] * len(earlier),
        out_specs=[mine] * 3 + [pl.BlockSpec((part, width), lambda i: (0, 0))],
        out_shape=[whole] * 3 + [jax.ShapeDtypeStruct((part, width), bf16)],
        input_output_aliases={RING + 3 + i: i for i in range(len(earlier))},
        compiler_params=params("arbitrary"),
        cost_estimate=pl.CostEstimate(flops=2_000_000, bytes_accessed=4_000_000, transcendentals=rows * width),
        name="adam",
    )(*pieces, *state, *earlier)


def by_slot(next_map, pieces):
    def kernel(map_ref, *refs):
        ins, outs = refs[:RING], refs[RING:]
        slot = lax.axis_index("slot")
        y, z = slot // RING, slot % RING
        for distance in range(RING):
            wanted = (map_ref[RING * y + (z + distance) % RING] - y + RING) % RING
            for step in range(RING):

                @pl.when(wanted == step)
                def _(step=step, distance=distance):
                    outs[distance][...] = ins[step][...]

    shape = pieces[0].shape
    return pl.pallas_call(
        kernel,
        grid_spec=pltpu.PrefetchScalarGridSpec(
            num_scalar_prefetch=1,
            grid=(1,),
            in_specs=[pl.BlockSpec(shape, lambda i, m: (0, 0))] * RING,
            out_specs=[pl.BlockSpec(shape, lambda i, m: (0, 0))] * RING,
        ),
        out_shape=[jax.ShapeDtypeStruct(shape, bf16)] * RING,
        compiler_params=params("arbitrary"),
        cost_estimate=pl.CostEstimate(flops=0, bytes_accessed=2_000_000, transcendentals=0),
        name="by_slot",
    )(next_map, *pieces)


def put_rows(place, chunk, pieces, ff, earlier):
    part, width = pieces[0].shape

    def kernel(place_ref, *refs):
        out = refs[-1]
        for distance in range(RING):

            @pl.when(pl.program_id(0) == distance)
            def _(distance=distance):
                out[...] = refs[distance][...]

    return pl.pallas_call(
        kernel,
        grid_spec=pltpu.PrefetchScalarGridSpec(
            num_scalar_prefetch=1,
            grid=(RING,),
            in_specs=[pl.BlockSpec((part, width), lambda i, p: (0, 0))] * RING
            + [pl.BlockSpec(memory_space=pl.ANY)] * len(earlier),
            out_specs=pl.BlockSpec((part, width), lambda i, p: (((p[3] + i) % RING) * CHUNKS + chunk, 0)),
        ),
        out_shape=jax.ShapeDtypeStruct((ff, width), bf16),
        input_output_aliases={1 + RING: 0} if earlier else {},
        compiler_params=params("arbitrary"),
        cost_estimate=pl.CostEstimate(flops=0, bytes_accessed=2_000_000, transcendentals=0),
        name="put_rows",
    )(place, *pieces, *earlier)


def local(acts, out_grads, counts, replica_map, next_map, slot_weights, master, moment1, moment2):
    hidden, grads, weight = acts[0], out_grads[0], slot_weights[0]
    ff = hidden.shape[1]
    scale = ff**-0.5
    slot, shard = lax.axis_index("slot"), lax.axis_index("shard")
    place = jnp.stack([shard // 2, shard % 2, counts[0], slot % RING]).astype(jnp.int32)

    other_weight, other_grads = swap_core(weight), swap_core(grads)
    by_chunk = slot_grads(counts, hidden, grads, scale)
    along_z = [exchange(shift_z, pieces) for pieces in by_chunk]

    halves = []
    for half in range(2):
        terms = act_terms(place, half, 2, grads, other_grads, weight, other_weight, scale)
        halves.append(exchange(shift_x, terms))

    along_y = [exchange(shift_y, by_expert(replica_map, pieces)) for pieces in along_z]
    state = ()
    fresh = []
    for chunk, pieces in enumerate(along_y):
        *state, rows = adam(chunk, pieces, (master, moment1, moment2), tuple(state))
        fresh.append(exchange(shift_y, [rows] * RING))
    wanted = [exchange(shift_z, by_slot(next_map, pieces)) for pieces in fresh]
    new_weight = ()
    for chunk, pieces in enumerate(wanted):
        new_weight = (put_rows(place, chunk, pieces, ff, new_weight),)
    act_grads = act_sum(halves)
    return (new_weight[0][None], *state, act_grads[None])


def solution(mesh):
    placed = (
        P("slot", None, None),
        P("slot", None, "shard"),
        P("slot"),
        P(),
        P(),
        P("slot", None, "shard"),
        P("slot", "shard"),
        P("slot", "shard"),
        P("slot", "shard"),
    )
    return jax.shard_map(
        local,
        mesh=mesh,
        in_specs=placed,
        out_specs=(
            P("slot", None, "shard"),
            P("slot", "shard"),
            P("slot", "shard"),
            P("slot", "shard"),
            P("slot", None, "shard"),
        ),
        check_vma=False,
    )
```

```python
import functools

import jax
import jax.numpy as jnp
from jax import lax
from jax.experimental import pallas as pl
from jax.experimental.pallas import tpu as pltpu
from jax.sharding import PartitionSpec as P

beta_one = 0.9
beta_two = 0.95
learn_rate = 0.5
weight_decay = 0.1
epsilon = 1e-08
adam_step = 20

RING = 4
CHUNKS = 2
bf16 = jnp.bfloat16
f32 = jnp.float32


def params(limit, *semantics):
    return pltpu.CompilerParams(vmem_limit_bytes=int(limit * 2**20), dimension_semantics=semantics or None)


VMEM = pl.BlockSpec(memory_space=pltpu.VMEM)
SMEM = pl.BlockSpec(memory_space=pltpu.SMEM)
ANY = pl.BlockSpec(memory_space=pl.ANY)
HBM = pl.BlockSpec(memory_space=pltpu.HBM)


def turned(distance, core):
    return distance ^ ((distance & 1) * 2 * core)


def along(stride):
    def move(value, distance):
        pairs = [
            (slot * 2 * RING + shard, (slot ^ (turned(distance, shard % 2) * stride)) * 2 * RING + shard)
            for slot in range(RING * RING)
            for shard in range(2 * RING)
        ]
        return lax.ppermute(value, ("slot", "shard"), pairs)

    return move


move_z = along(1)
move_y = along(RING)


def exchange(move, pieces):
    return [pieces[0]] + [move(pieces[distance], distance) for distance in range(1, RING)]


def my_place():
    slot = lax.axis_index("slot")
    return slot // RING, slot % RING, lax.axis_index("shard") % 2


def slot_grads(counts, acts, out_grads, scale):
    tokens, ff = acts.shape
    width = out_grads.shape[1]
    quarter = ff // RING
    part = quarter // CHUNKS
    blocks = [256, 512, 768, 768, 768]
    starts = [sum(blocks[:i]) for i in range(len(blocks))]
    assert sum(blocks) == tokens

    def kernel(count_ref, acts_hbm, grads_hbm, *rest):
        outs, (acts_ref, grads_ref, total, sems) = rest[:-4], rest[-4:]
        _, z, core = my_place()
        copies = []
        for i, (start, block) in enumerate(zip(starts, blocks)):
            rows = pl.ds(start, block)
            copies.append(
                (
                    pltpu.make_async_copy(grads_hbm.at[rows, :], grads_ref.at[rows, :], sems.at[2 * i]),
                    pltpu.make_async_copy(acts_hbm.at[rows, :], acts_ref.at[rows, :], sems.at[2 * i + 1]),
                )
            )
        for pair in copies:
            for copy in pair:
                copy.start()
        for i, (start, block) in enumerate(zip(starts, blocks)):
            for copy in copies[i]:
                copy.wait()
            rows = lax.broadcasted_iota(jnp.int32, (block, width), 0)
            grads = grads_ref[start : start + block, :]
            masked = jnp.where(rows < count_ref[0] - start, grads, jnp.zeros_like(grads))
            term = lax.dot_general(
                masked, acts_ref[start : start + block, :], (((0,), (0,)), ((), ())), preferred_element_type=f32
            )
            total[...] = term if i == 0 else total[...] + term
        for chunk in range(CHUNKS):
            for distance in range(RING):
                start = (z ^ turned(distance, core)) * quarter + chunk * part
                columns = total[:, pl.ds(pl.multiple_of(start, part), part)]
                outs[chunk * RING + distance][...] = (columns * scale).astype(bf16)

    pieces = pl.pallas_call(
        kernel,
        in_specs=[SMEM, HBM, HBM],
        out_specs=[VMEM] * (CHUNKS * RING),
        out_shape=[jax.ShapeDtypeStruct((width, part), bf16)] * (CHUNKS * RING),
        scratch_shapes=[
            pltpu.VMEM((tokens, ff), bf16),
            pltpu.VMEM((tokens, width), bf16),
            pltpu.VMEM((width, ff), f32),
            pltpu.SemaphoreType.DMA((2 * len(blocks),)),
        ],
        compiler_params=params(57.5),
        cost_estimate=pl.CostEstimate(flops=2 * tokens * ff * width, bytes_accessed=14_000_000, transcendentals=0),
        name="slot_grads",
    )(counts, acts, out_grads)
    return [pieces[chunk * RING : (chunk + 1) * RING] for chunk in range(CHUNKS)]


def act_terms(counts, out_grads, weight, scale, after):
    tokens, width = out_grads.shape
    ff = weight.shape[0]
    block = 512
    steps = tokens // block
    columns = ff // (2 * RING)

    def kernel(count_ref, grads_ref, weight_ref, after_ref, out_ref, done_ref):
        live = count_ref[0] - pl.program_id(0) * block
        term = lax.dot_general(grads_ref[...], weight_ref[...], (((1,), (1,)), ((), ())), preferred_element_type=f32)
        rows = lax.broadcasted_iota(jnp.int32, term.shape, 0)
        term = jnp.where(rows < live, term * scale, 0.0).astype(bf16)
        for piece in range(2 * RING):
            out_ref[piece] = term[:, piece * columns : (piece + 1) * columns]
        done_ref[0] = 0

    return pl.pallas_call(
        kernel,
        grid_spec=pltpu.PrefetchScalarGridSpec(
            num_scalar_prefetch=1,
            grid=(steps,),
            in_specs=[
                pl.BlockSpec((block, width), lambda i, c: (i, 0)),
                pl.BlockSpec((ff, width), lambda i, c: (0, 0)),
                ANY,
            ],
            out_specs=[
                pl.BlockSpec((2 * RING, block, columns), lambda i, c: (0, i, 0)),
                SMEM,
            ],
        ),
        out_shape=[jax.ShapeDtypeStruct((2 * RING, tokens, columns), bf16), jax.ShapeDtypeStruct((1,), jnp.int32)],
        compiler_params=params(50, "arbitrary"),
        cost_estimate=pl.CostEstimate(flops=2 * tokens * ff * width, bytes_accessed=14_000_000, transcendentals=0),
        name="act_terms",
    )(counts, out_grads, weight, after)


def by_expert(replica_map, pieces, after):
    def kernel(map_ref, after_ref, *refs):
        ins, outs = refs[:RING], refs[RING:]
        y, z, core = my_place()
        values = [ref[...].astype(f32) for ref in ins]
        held = [map_ref[RING * y + (z ^ turned(distance, core))] for distance in range(RING)]
        for step in range(RING):
            expert = y ^ turned(step, core)
            total = jnp.where(held[0] == expert, values[0], 0.0)
            for value, one in zip(values[1:], held[1:]):
                total = total + jnp.where(one == expert, value, 0.0)
            outs[step][...] = total.astype(bf16)

    shape = pieces[0].shape
    return pl.pallas_call(
        kernel,
        in_specs=[SMEM, SMEM] + [VMEM] * RING,
        out_specs=[VMEM] * RING,
        out_shape=[jax.ShapeDtypeStruct(shape, bf16)] * RING,
        compiler_params=params(16),
        cost_estimate=pl.CostEstimate(flops=1_000_000, bytes_accessed=2_000_000, transcendentals=0),
        name="by_expert",
    )(replica_map, after, *pieces)


def adam_update(grad_total, master, moment1, moment2):
    new_first = beta_one * moment1 + (1.0 - beta_one) * grad_total
    new_second = beta_two * moment2 + (1.0 - beta_two) * grad_total * grad_total
    first_hat = new_first / (1.0 - beta_one**adam_step)
    second_hat = new_second / (1.0 - beta_two**adam_step)
    update = first_hat / (jnp.sqrt(second_hat) + epsilon)
    master_new = master - learn_rate * (update + weight_decay * master)
    return (master_new, new_first, new_second)


def adam(chunk, pieces, state, earlier):
    rows, width = state[0].shape
    part = rows // CHUNKS

    def kernel(*refs):
        terms = [ref[...].astype(f32) for ref in refs[:RING]]
        master, moment1, moment2 = refs[RING : RING + 3]
        outs = refs[-4:]
        grad = ((terms[0] + terms[1]) + (terms[2] + terms[3])).T
        master_new, new_first, new_second = adam_update(grad, master[...], moment1[...], moment2[...])
        outs[0][...] = master_new
        outs[1][...] = new_first
        outs[2][...] = new_second
        outs[3][...] = master_new.astype(bf16)

    whole = jax.ShapeDtypeStruct((rows, width), f32)
    mine = pl.BlockSpec((part, width), lambda i: (chunk, 0))
    return pl.pallas_call(
        kernel,
        grid=(1,),
        in_specs=[VMEM] * RING + [mine] * 3 + [ANY] * len(earlier),
        out_specs=[mine] * 3 + [VMEM],
        out_shape=[whole] * 3 + [jax.ShapeDtypeStruct((part, width), bf16)],
        input_output_aliases={RING + 3 + i: i for i in range(len(earlier))},
        compiler_params=params(16, "arbitrary"),
        cost_estimate=pl.CostEstimate(flops=2_000_000, bytes_accessed=4_000_000, transcendentals=rows * width),
        name="adam",
    )(*pieces, *state, *earlier)


def by_slot(next_map, pieces):
    def kernel(map_ref, *refs):
        ins, outs = refs[:RING], refs[RING:]
        y, z, core = my_place()
        for distance in range(RING):
            wanted = turned(map_ref[RING * y + (z ^ turned(distance, core))] ^ y, core)
            for step in range(RING):

                @pl.when(wanted == step)
                def _(step=step, distance=distance):
                    outs[distance][...] = ins[step][...]

    shape = pieces[0].shape
    return pl.pallas_call(
        kernel,
        in_specs=[SMEM] + [VMEM] * RING,
        out_specs=[VMEM] * RING,
        out_shape=[jax.ShapeDtypeStruct(shape, bf16)] * RING,
        compiler_params=params(16),
        cost_estimate=pl.CostEstimate(flops=0, bytes_accessed=2_000_000, transcendentals=0),
        name="by_slot",
    )(next_map, *pieces)


def put_rows(chunk, pieces, ff, earlier):
    part, width = pieces[0].shape

    def kernel(*refs):
        ins, out, sems = refs[:RING], refs[-2], refs[-1]
        _, z, core = my_place()
        copies = []
        for distance in range(RING):
            start = (z ^ turned(distance, core)) * (part * CHUNKS) + chunk * part
            target = out.at[pl.ds(pl.multiple_of(start, part), part), :]
            copies.append(pltpu.make_async_copy(ins[distance], target, sems.at[distance]))
        for copy in copies:
            copy.start()
        for copy in copies:
            copy.wait()

    return pl.pallas_call(
        kernel,
        in_specs=[VMEM] * RING + [ANY] * len(earlier),
        out_specs=ANY,
        out_shape=jax.ShapeDtypeStruct((ff, width), bf16),
        scratch_shapes=[pltpu.SemaphoreType.DMA((RING,))],
        input_output_aliases={RING: 0} if earlier else {},
        compiler_params=params(16),
        cost_estimate=pl.CostEstimate(flops=0, bytes_accessed=2_000_000, transcendentals=0),
        name="put_rows",
    )(*pieces, *earlier)


def local(acts, out_grads, counts, replica_map, next_map, slot_weights, master, moment1, moment2):
    hidden, grads, weight = acts[0], out_grads[0], slot_weights[0]
    ff = hidden.shape[1]
    scale = ff**-0.5

    by_chunk = slot_grads(counts, hidden, grads, scale)
    along_z = [exchange(move_z, by_chunk[0])]
    terms, after = act_terms(counts, grads, weight, scale, by_chunk[0][0])
    terms, later, _ = lax.optimization_barrier((terms, by_chunk[1], along_z[0][1:]))
    act_grads = lax.psum_scatter(terms, "shard", scatter_dimension=0, tiled=False)
    along_z.append(exchange(move_z, later))
    along_y = [exchange(move_y, by_expert(replica_map, pieces, after)) for pieces in along_z]

    state = ()
    fresh = []
    for chunk, pieces in enumerate(along_y):
        *state, rows = adam(chunk, pieces, (master, moment1, moment2), tuple(state))
        fresh.append(exchange(move_y, [rows] * RING))
    wanted = [exchange(move_z, by_slot(next_map, pieces)) for pieces in fresh]
    new_weight = ()
    for chunk, pieces in enumerate(wanted):
        new_weight = (put_rows(chunk, pieces, ff, new_weight),)
    return (new_weight[0][None], *state, act_grads[None])


def solution(mesh):
    placed = (
        P("slot", None, None),
        P("slot", None, "shard"),
        P("slot"),
        P(),
        P(),
        P("slot", None, "shard"),
        P("slot", "shard"),
        P("slot", "shard"),
        P("slot", "shard"),
    )
    return jax.shard_map(
        local,
        mesh=mesh,
        in_specs=placed,
        out_specs=(
            P("slot", None, "shard"),
            P("slot", "shard"),
            P("slot", "shard"),
            P("slot", "shard"),
            P("slot", None, "shard"),
        ),
        check_vma=False,
    )
```

```python
import functools

import jax
import jax.numpy as jnp
from jax import lax
from jax.experimental import pallas as pl
from jax.experimental.pallas import tpu as pltpu
from jax.sharding import PartitionSpec as P

beta_one = 0.9
beta_two = 0.95
learn_rate = 0.5
weight_decay = 0.1
epsilon = 1e-08
adam_step = 20

RING = 4
CHUNKS = 2
bf16 = jnp.bfloat16
f32 = jnp.float32


def params(limit, *semantics):
    return pltpu.CompilerParams(vmem_limit_bytes=int(limit * 2**20), dimension_semantics=semantics or None)


BUSY = pl.CostEstimate(flops=10_000_000_000, bytes_accessed=14_000_000, transcendentals=0)
BRIEF = pl.CostEstimate(flops=0, bytes_accessed=1024, transcendentals=0)
TURN = jax.ShapeDtypeStruct((1,), jnp.int32)
VMEM = pl.BlockSpec(memory_space=pltpu.VMEM)
SMEM = pl.BlockSpec(memory_space=pltpu.SMEM)
ANY = pl.BlockSpec(memory_space=pl.ANY)
HBM = pl.BlockSpec(memory_space=pltpu.HBM)


def turned(distance, core):
    return distance ^ ((distance & 1) * 2 * core)


def along(stride):
    def move(value, distance):
        pairs = [
            (slot * 2 * RING + shard, (slot ^ (turned(distance, shard % 2) * stride)) * 2 * RING + shard)
            for slot in range(RING * RING)
            for shard in range(2 * RING)
        ]
        return lax.ppermute(value, ("slot", "shard"), pairs)

    return move


move_z = along(1)
move_y = along(RING)


def exchange(move, pieces):
    return [pieces[0]] + [move(pieces[distance], distance) for distance in range(1, RING)]


def my_place():
    slot = lax.axis_index("slot")
    return slot // RING, slot % RING, lax.axis_index("shard") % 2


def slot_grads(chunk, counts, acts, out_grads, scale, after):
    tokens, ff = acts.shape
    width = out_grads.shape[1]
    quarter = ff // RING
    part = quarter // CHUNKS
    blocks = [256, 512, 768, 768, 768]
    starts = [sum(blocks[:i]) for i in range(len(blocks))]
    assert sum(blocks) == tokens

    def kernel(count_ref, acts_hbm, grads_hbm, *rest):
        outs, (acts_ref, grads_ref, total, sems) = rest[-4 - RING : -4], rest[-4:]
        _, z, core = my_place()
        copies = []
        for i, (start, block) in enumerate(zip(starts, blocks)):
            rows = pl.ds(start, block)
            group = [pltpu.make_async_copy(grads_hbm.at[rows, :], grads_ref.at[rows, :], sems.at[i, RING])]
            for distance in range(RING):
                column = pl.multiple_of((z ^ turned(distance, core)) * quarter + chunk * part, part)
                source = acts_hbm.at[rows, pl.ds(column, part)]
                target = acts_ref.at[rows, pl.ds(distance * part, part)]
                group.append(pltpu.make_async_copy(source, target, sems.at[i, distance]))
            copies.append(group)
        for group in copies:
            for copy in group:
                copy.start()
        for i, (start, block) in enumerate(zip(starts, blocks)):
            for copy in copies[i]:
                copy.wait()
            rows = lax.broadcasted_iota(jnp.int32, (block, width), 0)
            grads = grads_ref[start : start + block, :]
            masked = jnp.where(rows < count_ref[0] - start, grads, jnp.zeros_like(grads))
            term = lax.dot_general(
                acts_ref[start : start + block, :], masked, (((0,), (0,)), ((), ())), preferred_element_type=f32
            )
            if i < len(blocks) - 1:
                total[...] = term if i == 0 else total[...] + term
            else:
                term = ((total[...] + term) * scale).astype(bf16)
                for distance in range(RING):
                    outs[distance][...] = term[distance * part : (distance + 1) * part, :]

    return pl.pallas_call(
        kernel,
        in_specs=[SMEM, HBM, HBM] + [ANY] * len(after),
        out_specs=[VMEM] * RING,
        out_shape=[jax.ShapeDtypeStruct((part, width), bf16)] * RING,
        scratch_shapes=[
            pltpu.VMEM((tokens, RING * part), bf16),
            pltpu.VMEM((tokens, width), bf16),
            pltpu.VMEM((RING * part, width), f32),
            pltpu.SemaphoreType.DMA((len(blocks), RING + 1)),
        ],
        compiler_params=params(57.25),
        cost_estimate=BUSY,
        name="slot_grads",
    )(counts, acts, out_grads, *after)


def act_terms(counts, out_grads, weight, scale, after):
    tokens, width = out_grads.shape
    ff = weight.shape[0]
    block = 1024
    steps = tokens // block
    columns = ff // (2 * RING)

    def kernel(count_ref, grads_ref, weight_ref, *rest):
        out_ref, turn_ref = rest[-2:]
        turn_ref[0] = 0
        live = count_ref[0] - pl.program_id(0) * block
        term = lax.dot_general(grads_ref[...], weight_ref[...], (((1,), (1,)), ((), ())), preferred_element_type=f32)
        rows = lax.broadcasted_iota(jnp.int32, term.shape, 0)
        term = jnp.where(rows < live, term * scale, 0.0).astype(bf16)
        for piece in range(2 * RING):
            out_ref[piece] = term[:, piece * columns : (piece + 1) * columns]

    return pl.pallas_call(
        kernel,
        grid_spec=pltpu.PrefetchScalarGridSpec(
            num_scalar_prefetch=1,
            grid=(steps,),
            in_specs=[
                pl.BlockSpec((block, width), lambda i, c: (i, 0)),
                pl.BlockSpec((ff, width), lambda i, c: (0, 0)),
            ]
            + [ANY] * len(after),
            out_specs=[pl.BlockSpec((2 * RING, block, columns), lambda i, c: (0, i, 0)), SMEM],
        ),
        out_shape=[jax.ShapeDtypeStruct((2 * RING, tokens, columns), bf16), TURN],
        compiler_params=params(50, "arbitrary"),
        cost_estimate=BUSY,
        name="act_terms",
    )(counts, out_grads, weight, *after)


def by_expert(replica_map, pieces, after=(), behind=()):
    shape = pieces[0].shape

    def kernel(map_ref, *refs):
        ins, outs = refs[:RING], refs[-RING:]
        y, z, core = my_place()
        values = [ref[...].astype(f32) for ref in ins]
        held = [map_ref[RING * y + (z ^ turned(distance, core))] for distance in range(RING)]
        for step in range(RING):
            expert = y ^ turned(step, core)
            total = jnp.where(held[0] == expert, values[0], 0.0)
            for value, one in zip(values[1:], held[1:]):
                total = total + jnp.where(one == expert, value, 0.0)
            outs[step][...] = total.astype(bf16)

    return pl.pallas_call(
        kernel,
        in_specs=[SMEM] + [VMEM] * RING + [SMEM] * len(after) + [ANY] * len(behind),
        out_specs=[VMEM] * RING,
        out_shape=[jax.ShapeDtypeStruct(shape, bf16)] * RING,
        compiler_params=params(16),
        cost_estimate=BRIEF,
        name="by_expert",
    )(replica_map, *pieces, *after, *behind)


def adam_update(grad_total, master, moment1, moment2):
    new_first = beta_one * moment1 + (1.0 - beta_one) * grad_total
    new_second = beta_two * moment2 + (1.0 - beta_two) * grad_total * grad_total
    first_hat = new_first / (1.0 - beta_one**adam_step)
    second_hat = new_second / (1.0 - beta_two**adam_step)
    update = first_hat / (jnp.sqrt(second_hat) + epsilon)
    master_new = master - learn_rate * (update + weight_decay * master)
    return (master_new, new_first, new_second)


def adam(chunk, pieces, state, earlier, turns=0, behind=()):
    rows, width = state[0].shape
    part = rows // CHUNKS

    def kernel(*refs):
        terms = [ref[...].astype(f32) for ref in refs[:RING]]
        master, moment1, moment2 = refs[RING : RING + 3]
        outs = refs[-4 - turns :]
        if turns:
            outs[4][0] = 0
        grad = (terms[0] + terms[1]) + (terms[2] + terms[3])
        master_new, new_first, new_second = adam_update(grad, master[...], moment1[...], moment2[...])
        outs[0][...] = master_new
        outs[1][...] = new_first
        outs[2][...] = new_second
        outs[3][...] = master_new.astype(bf16)

    whole = jax.ShapeDtypeStruct((rows, width), f32)
    mine = pl.BlockSpec((part, width), lambda i: (chunk, 0))
    return pl.pallas_call(
        kernel,
        grid=(1,),
        in_specs=[pl.BlockSpec((part, width), lambda i: (0, 0))] + [VMEM] * (RING - 1) + [mine] * 3 + [ANY] * (len(earlier) + len(behind)),
        out_specs=[mine] * 3 + [VMEM] + [SMEM] * turns,
        out_shape=[whole] * 3 + [jax.ShapeDtypeStruct((part, width), bf16)] + [TURN] * turns,
        input_output_aliases={RING + 3 + i: i for i in range(len(earlier))},
        compiler_params=params(16, "arbitrary"),
        cost_estimate=BRIEF,
        name="adam",
    )(*pieces, *state, *earlier, *behind)


def by_slot(next_map, pieces):
    def kernel(map_ref, *refs):
        ins, outs = refs[:RING], refs[RING:]
        y, z, core = my_place()
        for distance in range(RING):
            wanted = turned(map_ref[RING * y + (z ^ turned(distance, core))] ^ y, core)
            for step in range(RING):

                @pl.when(wanted == step)
                def _(step=step, distance=distance):
                    outs[distance][...] = ins[step][...]

    shape = pieces[0].shape
    return pl.pallas_call(
        kernel,
        in_specs=[SMEM] + [VMEM] * RING,
        out_specs=[VMEM] * RING,
        out_shape=[jax.ShapeDtypeStruct(shape, bf16)] * RING,
        compiler_params=params(16),
        cost_estimate=BRIEF,
        name="by_slot",
    )(next_map, *pieces)


def put_rows(chunk, pieces, ff, earlier, after=()):
    part, width = pieces[0].shape

    def kernel(*refs):
        ins, out, sems = refs[:RING], refs[-2], refs[-1]
        _, z, core = my_place()
        copies = []
        for distance in range(RING):
            start = (z ^ turned(distance, core)) * (part * CHUNKS) + chunk * part
            target = out.at[pl.ds(pl.multiple_of(start, part), part), :]
            copies.append(pltpu.make_async_copy(ins[distance], target, sems.at[distance]))
        for copy in copies:
            copy.start()
        for copy in copies:
            copy.wait()

    return pl.pallas_call(
        kernel,
        in_specs=[VMEM] * RING + [ANY] * len(earlier) + [SMEM] * len(after),
        out_specs=ANY,
        out_shape=jax.ShapeDtypeStruct((ff, width), bf16),
        scratch_shapes=[pltpu.SemaphoreType.DMA((RING,))],
        input_output_aliases={RING: 0} if earlier else {},
        compiler_params=params(16),
        cost_estimate=BRIEF,
        name="put_rows",
    )(*pieces, *earlier, *after)


def local(acts, out_grads, counts, replica_map, next_map, slot_weights, master, moment1, moment2):
    hidden, grads, weight = acts[0], out_grads[0], slot_weights[0]
    ff = hidden.shape[1]
    scale = ff**-0.5

    first = slot_grads(0, counts, hidden, grads, scale, ())
    second = slot_grads(1, counts, hidden, grads, scale, first[:1])
    along_z = [exchange(move_z, first), exchange(move_z, second)]
    sums = by_expert(replica_map, along_z[0])
    early = exchange(move_y, sums)
    terms, turn = act_terms(counts, grads, weight, scale, (sums[0], second[0]))
    sums = by_expert(replica_map, along_z[1], (turn,), early[1:])
    late = exchange(move_y, sums)
    *state, rows, turn = adam(0, early, (master, moment1, moment2), (), 1, sums[:1])
    terms, turn = lax.optimization_barrier((terms, turn))
    act_grads = lax.psum_scatter(terms, "shard", scatter_dimension=0, tiled=False)
    fresh = [exchange(move_y, [rows] * RING)]
    *state, rows = adam(1, late, (master, moment1, moment2), tuple(state))
    fresh.append(exchange(move_y, [rows] * RING))
    wanted = [exchange(move_z, by_slot(next_map, pieces)) for pieces in fresh]
    new_weight = put_rows(0, wanted[0], ff, (), (turn,))
    new_weight = put_rows(1, wanted[1], ff, (new_weight,))
    return (new_weight[None], *state, act_grads[None])


def solution(mesh):
    placed = (
        P("slot", None, None),
        P("slot", None, "shard"),
        P("slot"),
        P(),
        P(),
        P("slot", None, "shard"),
        P("slot", "shard"),
        P("slot", "shard"),
        P("slot", "shard"),
    )
    return jax.shard_map(
        local,
        mesh=mesh,
        in_specs=placed,
        out_specs=(
            P("slot", None, "shard"),
            P("slot", "shard"),
            P("slot", "shard"),
            P("slot", "shard"),
            P("slot", None, "shard"),
        ),
        check_vma=False,
    )
```

```python
import functools

import jax
import jax.numpy as jnp
from jax import lax
from jax.experimental import pallas as pl
from jax.experimental.pallas import tpu as pltpu
from jax.sharding import PartitionSpec as P

beta_one = 0.9
beta_two = 0.95
learn_rate = 0.5
weight_decay = 0.1
epsilon = 1e-08
adam_step = 20

RING = 4
CHUNKS = 2
bf16 = jnp.bfloat16
f32 = jnp.float32


def params(limit, *semantics):
    return pltpu.CompilerParams(vmem_limit_bytes=int(limit * 2**20), dimension_semantics=semantics or None)


BUSY = pl.CostEstimate(flops=10_000_000_000, bytes_accessed=14_000_000, transcendentals=0)
BRIEF = pl.CostEstimate(flops=0, bytes_accessed=1024, transcendentals=0)
TURN = jax.ShapeDtypeStruct((1,), jnp.int32)
VMEM = pl.BlockSpec(memory_space=pltpu.VMEM)
SMEM = pl.BlockSpec(memory_space=pltpu.SMEM)
ANY = pl.BlockSpec(memory_space=pl.ANY)
HBM = pl.BlockSpec(memory_space=pltpu.HBM)


def turned(distance, core):
    return distance ^ ((distance & 1) * 2 * core)


def along(stride):
    def move(value, distance):
        pairs = [
            (slot * 2 * RING + shard, (slot ^ (turned(distance, shard % 2) * stride)) * 2 * RING + shard)
            for slot in range(RING * RING)
            for shard in range(2 * RING)
        ]
        return lax.ppermute(value, ("slot", "shard"), pairs)

    return move


move_z = along(1)
move_y = along(RING)


def exchange(move, pieces):
    return [pieces[0]] + [move(pieces[distance], distance) for distance in range(1, RING)]


def my_place():
    slot = lax.axis_index("slot")
    return slot // RING, slot % RING, lax.axis_index("shard") % 2


def slot_grads(chunk, counts, acts, out_grads, scale, after):
    tokens, ff = acts.shape
    width = out_grads.shape[1]
    quarter = ff // RING
    part = quarter // CHUNKS
    blocks = [256, 512, 768, 768, 768]
    starts = [sum(blocks[:i]) for i in range(len(blocks))]
    assert sum(blocks) == tokens

    def kernel(count_ref, acts_hbm, grads_hbm, *rest):
        outs, (acts_ref, grads_ref, total, sems) = rest[-4 - RING : -4], rest[-4:]
        _, z, core = my_place()
        copies = []
        for i, (start, block) in enumerate(zip(starts, blocks)):
            rows = pl.ds(start, block)
            group = [pltpu.make_async_copy(grads_hbm.at[rows, :], grads_ref.at[rows, :], sems.at[i, RING])]
            for distance in range(RING):
                column = pl.multiple_of((z ^ turned(distance, core)) * quarter + chunk * part, part)
                source = acts_hbm.at[rows, pl.ds(column, part)]
                target = acts_ref.at[rows, pl.ds(distance * part, part)]
                group.append(pltpu.make_async_copy(source, target, sems.at[i, distance]))
            copies.append(group)
        for group in copies:
            for copy in group:
                copy.start()
        for i, (start, block) in enumerate(zip(starts, blocks)):
            for copy in copies[i]:
                copy.wait()
            rows = lax.broadcasted_iota(jnp.int32, (block, width), 0)
            grads = grads_ref[start : start + block, :]
            masked = jnp.where(rows < count_ref[0] - start, grads, jnp.zeros_like(grads))
            term = lax.dot_general(
                acts_ref[start : start + block, :], masked, (((0,), (0,)), ((), ())), preferred_element_type=f32
            )
            if i < len(blocks) - 1:
                total[...] = term if i == 0 else total[...] + term
            else:
                term = ((total[...] + term) * scale).astype(bf16)
                for distance in range(RING):
                    outs[distance][...] = term[distance * part : (distance + 1) * part, :]

    return pl.pallas_call(
        kernel,
        in_specs=[SMEM, HBM, HBM] + [ANY] * len(after),
        out_specs=[VMEM] * RING,
        out_shape=[jax.ShapeDtypeStruct((part, width), bf16)] * RING,
        scratch_shapes=[
            pltpu.VMEM((tokens, RING * part), bf16),
            pltpu.VMEM((tokens, width), bf16),
            pltpu.VMEM((RING * part, width), f32),
            pltpu.SemaphoreType.DMA((len(blocks), RING + 1)),
        ],
        compiler_params=params(57.25),
        cost_estimate=BUSY,
        name="slot_grads",
    )(counts, acts, out_grads, *after)


def act_terms(counts, out_grads, weight, scale, after):
    tokens, width = out_grads.shape
    ff = weight.shape[0]
    block = 1024
    steps = tokens // block
    columns = ff // (2 * RING)

    def kernel(count_ref, grads_ref, weight_ref, *rest):
        out_ref, turn_ref = rest[-2:]
        turn_ref[0] = 0
        live = count_ref[0] - pl.program_id(0) * block
        term = lax.dot_general(grads_ref[...], weight_ref[...], (((1,), (1,)), ((), ())), preferred_element_type=f32)
        rows = lax.broadcasted_iota(jnp.int32, term.shape, 0)
        term = jnp.where(rows < live, term * scale, 0.0).astype(bf16)
        for piece in range(2 * RING):
            out_ref[piece] = term[:, piece * columns : (piece + 1) * columns]

    return pl.pallas_call(
        kernel,
        grid_spec=pltpu.PrefetchScalarGridSpec(
            num_scalar_prefetch=1,
            grid=(steps,),
            in_specs=[
                pl.BlockSpec((block, width), lambda i, c: (i, 0)),
                pl.BlockSpec((ff, width), lambda i, c: (0, 0)),
            ]
            + [ANY] * len(after),
            out_specs=[pl.BlockSpec((2 * RING, block, columns), lambda i, c: (0, i, 0)), SMEM],
        ),
        out_shape=[jax.ShapeDtypeStruct((2 * RING, tokens, columns), bf16), TURN],
        compiler_params=params(50, "arbitrary"),
        cost_estimate=BUSY,
        name="act_terms",
    )(counts, out_grads, weight, *after)


def by_expert(replica_map, pieces, after=(), behind=()):
    shape = pieces[0].shape

    def kernel(map_ref, *refs):
        ins, outs = refs[:RING], refs[-RING:]
        y, z, core = my_place()
        values = [ref[...].astype(f32) for ref in ins]
        held = [map_ref[RING * y + (z ^ turned(distance, core))] for distance in range(RING)]
        for step in range(RING):
            expert = y ^ turned(step, core)
            total = jnp.where(held[0] == expert, values[0], 0.0)
            for value, one in zip(values[1:], held[1:]):
                total = total + jnp.where(one == expert, value, 0.0)
            outs[step][...] = total.astype(bf16)

    return pl.pallas_call(
        kernel,
        in_specs=[SMEM] + [VMEM] * RING + [SMEM] * len(after) + [ANY] * len(behind),
        out_specs=[VMEM] * RING,
        out_shape=[jax.ShapeDtypeStruct(shape, bf16)] * RING,
        compiler_params=params(16),
        cost_estimate=BRIEF,
        name="by_expert",
    )(replica_map, *pieces, *after, *behind)


def adam_update(grad_total, master, moment1, moment2):
    new_first = beta_one * moment1 + (1.0 - beta_one) * grad_total
    new_second = beta_two * moment2 + (1.0 - beta_two) * grad_total * grad_total
    first_hat = new_first / (1.0 - beta_one**adam_step)
    second_hat = new_second / (1.0 - beta_two**adam_step)
    update = first_hat / (jnp.sqrt(second_hat) + epsilon)
    master_new = master - learn_rate * (update + weight_decay * master)
    return (master_new, new_first, new_second)


def adam(chunk, pieces, state, earlier, turns=0, behind=()):
    rows, width = state[0].shape
    part = rows // CHUNKS

    def kernel(*refs):
        terms = [ref[...].astype(f32) for ref in refs[:RING]]
        master, moment1, moment2 = refs[RING : RING + 3]
        outs = refs[-4 - turns :]
        if turns:
            outs[4][0] = 0
        grad = (terms[0] + terms[1]) + (terms[2] + terms[3])
        master_new, new_first, new_second = adam_update(grad, master[...], moment1[...], moment2[...])
        outs[0][...] = master_new
        outs[1][...] = new_first
        outs[2][...] = new_second
        outs[3][...] = master_new.astype(bf16)

    whole = jax.ShapeDtypeStruct((rows, width), f32)
    mine = pl.BlockSpec((part, width), lambda i: (chunk, 0))
    return pl.pallas_call(
        kernel,
        grid=(1,),
        in_specs=[pl.BlockSpec((part, width), lambda i: (0, 0))] + [VMEM] * (RING - 1) + [mine] * 3 + [ANY] * (len(earlier) + len(behind)),
        out_specs=[mine] * 3 + [VMEM] + [SMEM] * turns,
        out_shape=[whole] * 3 + [jax.ShapeDtypeStruct((part, width), bf16)] + [TURN] * turns,
        input_output_aliases={RING + 3 + i: i for i in range(len(earlier))},
        compiler_params=params(16, "arbitrary"),
        cost_estimate=BRIEF,
        name="adam",
    )(*pieces, *state, *earlier, *behind)


def by_slot(next_map, pieces):
    def kernel(map_ref, *refs):
        ins, outs = refs[:RING], refs[RING:]
        y, z, core = my_place()
        for distance in range(RING):
            wanted = turned(map_ref[RING * y + (z ^ turned(distance, core))] ^ y, core)
            for step in range(RING):

                @pl.when(wanted == step)
                def _(step=step, distance=distance):
                    outs[distance][...] = ins[step][...]

    shape = pieces[0].shape
    return pl.pallas_call(
        kernel,
        in_specs=[SMEM] + [VMEM] * RING,
        out_specs=[VMEM] * RING,
        out_shape=[jax.ShapeDtypeStruct(shape, bf16)] * RING,
        compiler_params=params(16),
        cost_estimate=BRIEF,
        name="by_slot",
    )(next_map, *pieces)


def put_rows(chunk, pieces, ff, earlier, after=()):
    part, width = pieces[0].shape

    def kernel(*refs):
        ins, out, sems = refs[:RING], refs[-2], refs[-1]
        _, z, core = my_place()
        copies = []
        for distance in range(RING):
            start = (z ^ turned(distance, core)) * (part * CHUNKS) + chunk * part
            target = out.at[pl.ds(pl.multiple_of(start, part), part), :]
            copies.append(pltpu.make_async_copy(ins[distance], target, sems.at[distance]))
        for copy in copies:
            copy.start()
        for copy in copies:
            copy.wait()

    return pl.pallas_call(
        kernel,
        in_specs=[VMEM] * RING + [ANY] * len(earlier) + [SMEM] * len(after),
        out_specs=ANY,
        out_shape=jax.ShapeDtypeStruct((ff, width), bf16),
        scratch_shapes=[pltpu.SemaphoreType.DMA((RING,))],
        input_output_aliases={RING: 0} if earlier else {},
        compiler_params=params(16),
        cost_estimate=BRIEF,
        name="put_rows",
    )(*pieces, *earlier, *after)


def local(acts, out_grads, counts, replica_map, next_map, slot_weights, master, moment1, moment2):
    hidden, grads, weight = acts[0], out_grads[0], slot_weights[0]
    ff = hidden.shape[1]
    scale = ff**-0.5

    first = slot_grads(0, counts, hidden, grads, scale, ())
    second = slot_grads(1, counts, hidden, grads, scale, first[:1])
    along_z = [exchange(move_z, first), exchange(move_z, second)]
    sums = by_expert(replica_map, along_z[0])
    early = exchange(move_y, sums)
    terms, turn = act_terms(counts, grads, weight, scale, (sums[0], along_z[1][1]))
    sums = by_expert(replica_map, along_z[1], (turn,), early[1:])
    late = exchange(move_y, sums)
    *state, rows, turn = adam(0, early, (master, moment1, moment2), (), 1, sums[:1])
    terms, turn = lax.optimization_barrier((terms, turn))
    act_grads = lax.psum_scatter(terms, "shard", scatter_dimension=0, tiled=False)
    fresh = [exchange(move_y, [rows] * RING)]
    *state, rows = adam(1, late, (master, moment1, moment2), tuple(state))
    fresh.append(exchange(move_y, [rows] * RING))
    wanted = [exchange(move_z, by_slot(next_map, pieces)) for pieces in fresh]
    new_weight = put_rows(0, wanted[0], ff, (), (turn,))
    new_weight = put_rows(1, wanted[1], ff, (new_weight,))
    return (new_weight[None], *state, act_grads[None])


def solution(mesh):
    placed = (
        P("slot", None, None),
        P("slot", None, "shard"),
        P("slot"),
        P(),
        P(),
        P("slot", None, "shard"),
        P("slot", "shard"),
        P("slot", "shard"),
        P("slot", "shard"),
    )
    return jax.shard_map(
        local,
        mesh=mesh,
        in_specs=placed,
        out_specs=(
            P("slot", None, "shard"),
            P("slot", "shard"),
            P("slot", "shard"),
            P("slot", "shard"),
            P("slot", None, "shard"),
        ),
        check_vma=False,
    )
```

```python
import functools

import jax
import jax.numpy as jnp
from jax import lax
from jax.experimental import pallas as pl
from jax.experimental.pallas import tpu as pltpu
from jax.sharding import PartitionSpec as P

beta_one = 0.9
beta_two = 0.95
learn_rate = 0.5
weight_decay = 0.1
epsilon = 1e-08
adam_step = 20

RING = 4
CHUNKS = 2
bf16 = jnp.bfloat16
f32 = jnp.float32


def params(limit, *semantics):
    return pltpu.CompilerParams(vmem_limit_bytes=int(limit * 2**20), dimension_semantics=semantics or None)


BUSY = pl.CostEstimate(flops=10_000_000_000, bytes_accessed=14_000_000, transcendentals=0)
BRIEF = pl.CostEstimate(flops=0, bytes_accessed=1024, transcendentals=0)
TURN = jax.ShapeDtypeStruct((1,), jnp.int32)
VMEM = pl.BlockSpec(memory_space=pltpu.VMEM)
SMEM = pl.BlockSpec(memory_space=pltpu.SMEM)
ANY = pl.BlockSpec(memory_space=pl.ANY)
HBM = pl.BlockSpec(memory_space=pltpu.HBM)


def swapped(bits):
    return ((bits & 1) << 1) | (bits >> 1)


def turned(index, core):
    distance = swapped(index)
    return distance ^ ((distance & 1) * 2 * core)


def index_of(distance, core):
    return swapped(distance ^ ((distance & 1) * 2 * core))


def along(stride):
    def move(value, distance):
        pairs = [
            (slot * 2 * RING + shard, (slot ^ (turned(distance, shard % 2) * stride)) * 2 * RING + shard)
            for slot in range(RING * RING)
            for shard in range(2 * RING)
        ]
        return lax.ppermute(value, ("slot", "shard"), pairs)

    return move


move_z = along(1)
move_y = along(RING)


def exchange(move, pieces):
    return [pieces[0]] + [move(pieces[distance], distance) for distance in range(1, RING)]


def my_place():
    slot = lax.axis_index("slot")
    return slot // RING, slot % RING, lax.axis_index("shard") % 2


def slot_grads(chunk, counts, acts, out_grads, scale, after):
    tokens, ff = acts.shape
    width = out_grads.shape[1]
    quarter = ff // RING
    part = quarter // CHUNKS
    blocks = [256, 512, 768, 768, 768]
    starts = [sum(blocks[:i]) for i in range(len(blocks))]
    assert sum(blocks) == tokens

    def kernel(count_ref, acts_hbm, grads_hbm, *rest):
        outs, (acts_ref, grads_ref, total, sems) = rest[-4 - RING : -4], rest[-4:]
        _, z, core = my_place()
        copies = []
        for i, (start, block) in enumerate(zip(starts, blocks)):
            rows = pl.ds(start, block)
            group = [pltpu.make_async_copy(grads_hbm.at[rows, :], grads_ref.at[rows, :], sems.at[i, RING])]
            for distance in range(RING):
                column = pl.multiple_of((z ^ turned(distance, core)) * quarter + chunk * part, part)
                source = acts_hbm.at[rows, pl.ds(column, part)]
                target = acts_ref.at[rows, pl.ds(distance * part, part)]
                group.append(pltpu.make_async_copy(source, target, sems.at[i, distance]))
            copies.append(group)
        for group in copies:
            for copy in group:
                copy.start()
        for i, (start, block) in enumerate(zip(starts, blocks)):
            for copy in copies[i]:
                copy.wait()
            rows = lax.broadcasted_iota(jnp.int32, (block, width), 0)
            grads = grads_ref[start : start + block, :]
            masked = jnp.where(rows < count_ref[0] - start, grads, jnp.zeros_like(grads))
            term = lax.dot_general(
                acts_ref[start : start + block, :], masked, (((0,), (0,)), ((), ())), preferred_element_type=f32
            )
            if i < len(blocks) - 1:
                total[...] = term if i == 0 else total[...] + term
            else:
                term = ((total[...] + term) * scale).astype(bf16)
                for distance in range(RING):
                    outs[distance][...] = term[distance * part : (distance + 1) * part, :]

    return pl.pallas_call(
        kernel,
        in_specs=[SMEM, HBM, HBM] + [ANY] * len(after),
        out_specs=[VMEM] * RING,
        out_shape=[jax.ShapeDtypeStruct((part, width), bf16)] * RING,
        scratch_shapes=[
            pltpu.VMEM((tokens, RING * part), bf16),
            pltpu.VMEM((tokens, width), bf16),
            pltpu.VMEM((RING * part, width), f32),
            pltpu.SemaphoreType.DMA((len(blocks), RING + 1)),
        ],
        compiler_params=params(57.25),
        cost_estimate=BUSY,
        name="slot_grads",
    )(counts, acts, out_grads, *after)


def act_terms(counts, out_grads, weight, scale, after):
    tokens, width = out_grads.shape
    ff = weight.shape[0]
    block = 1024
    steps = tokens // block
    columns = ff // (2 * RING)

    def kernel(count_ref, grads_ref, weight_ref, *rest):
        out_ref, turn_ref = rest[-2:]
        turn_ref[0] = 0
        live = count_ref[0] - pl.program_id(0) * block
        term = lax.dot_general(grads_ref[...], weight_ref[...], (((1,), (1,)), ((), ())), preferred_element_type=f32)
        rows = lax.broadcasted_iota(jnp.int32, term.shape, 0)
        term = jnp.where(rows < live, term * scale, 0.0).astype(bf16)
        for piece in range(2 * RING):
            out_ref[piece] = term[:, piece * columns : (piece + 1) * columns]

    return pl.pallas_call(
        kernel,
        grid_spec=pltpu.PrefetchScalarGridSpec(
            num_scalar_prefetch=1,
            grid=(steps,),
            in_specs=[
                pl.BlockSpec((block, width), lambda i, c: (i, 0)),
                pl.BlockSpec((ff, width), lambda i, c: (0, 0)),
            ]
            + [ANY] * len(after),
            out_specs=[pl.BlockSpec((2 * RING, block, columns), lambda i, c: (0, i, 0)), SMEM],
        ),
        out_shape=[jax.ShapeDtypeStruct((2 * RING, tokens, columns), bf16), TURN],
        compiler_params=params(50, "arbitrary"),
        cost_estimate=BUSY,
        name="act_terms",
    )(counts, out_grads, weight, *after)


def by_expert(replica_map, pieces, after=(), behind=()):
    shape = pieces[0].shape

    def kernel(map_ref, *refs):
        ins, outs = refs[:RING], refs[-RING:]
        y, z, core = my_place()
        values = [ref[...].astype(f32) for ref in ins]
        held = [map_ref[RING * y + (z ^ turned(distance, core))] for distance in range(RING)]
        for step in range(RING):
            expert = y ^ turned(step, core)
            total = jnp.where(held[0] == expert, values[0], 0.0)
            for value, one in zip(values[1:], held[1:]):
                total = total + jnp.where(one == expert, value, 0.0)
            outs[step][...] = total.astype(bf16)

    return pl.pallas_call(
        kernel,
        in_specs=[SMEM] + [VMEM] * RING + [SMEM] * len(after) + [ANY] * len(behind),
        out_specs=[VMEM] * RING,
        out_shape=[jax.ShapeDtypeStruct(shape, bf16)] * RING,
        compiler_params=params(16),
        cost_estimate=BRIEF,
        name="by_expert",
    )(replica_map, *pieces, *after, *behind)


def adam_update(grad_total, master, moment1, moment2):
    new_first = beta_one * moment1 + (1.0 - beta_one) * grad_total
    new_second = beta_two * moment2 + (1.0 - beta_two) * grad_total * grad_total
    first_hat = new_first / (1.0 - beta_one**adam_step)
    second_hat = new_second / (1.0 - beta_two**adam_step)
    update = first_hat / (jnp.sqrt(second_hat) + epsilon)
    master_new = master - learn_rate * (update + weight_decay * master)
    return (master_new, new_first, new_second)


def adam(chunk, pieces, state, earlier, turns=0, behind=()):
    rows, width = state[0].shape
    part = rows // CHUNKS

    def kernel(*refs):
        terms = [ref[...].astype(f32) for ref in refs[:RING]]
        master, moment1, moment2 = refs[RING : RING + 3]
        outs = refs[-4 - turns :]
        if turns:
            outs[4][0] = 0
        grad = (terms[0] + terms[1]) + (terms[2] + terms[3])
        master_new, new_first, new_second = adam_update(grad, master[...], moment1[...], moment2[...])
        outs[0][...] = master_new
        outs[1][...] = new_first
        outs[2][...] = new_second
        outs[3][...] = master_new.astype(bf16)

    whole = jax.ShapeDtypeStruct((rows, width), f32)
    mine = pl.BlockSpec((part, width), lambda i: (chunk, 0))
    return pl.pallas_call(
        kernel,
        grid=(1,),
        in_specs=[pl.BlockSpec((part, width), lambda i: (0, 0))] + [VMEM] * (RING - 1) + [mine] * 3 + [ANY] * (len(earlier) + len(behind)),
        out_specs=[mine] * 3 + [VMEM] + [SMEM] * turns,
        out_shape=[whole] * 3 + [jax.ShapeDtypeStruct((part, width), bf16)] + [TURN] * turns,
        input_output_aliases={RING + 3 + i: i for i in range(len(earlier))},
        compiler_params=params(16, "arbitrary"),
        cost_estimate=BRIEF,
        name="adam",
    )(*pieces, *state, *earlier, *behind)


def by_slot(next_map, pieces):
    def kernel(map_ref, *refs):
        ins, outs = refs[:RING], refs[RING:]
        y, z, core = my_place()
        for distance in range(RING):
            wanted = index_of(map_ref[RING * y + (z ^ turned(distance, core))] ^ y, core)
            for step in range(RING):

                @pl.when(wanted == step)
                def _(step=step, distance=distance):
                    outs[distance][...] = ins[step][...]

    shape = pieces[0].shape
    return pl.pallas_call(
        kernel,
        in_specs=[SMEM] + [VMEM] * RING,
        out_specs=[VMEM] * RING,
        out_shape=[jax.ShapeDtypeStruct(shape, bf16)] * RING,
        compiler_params=params(16),
        cost_estimate=BRIEF,
        name="by_slot",
    )(next_map, *pieces)


def put_rows(chunk, pieces, ff, earlier, after=()):
    part, width = pieces[0].shape

    def kernel(*refs):
        ins, out, sems = refs[:RING], refs[-2], refs[-1]
        _, z, core = my_place()
        copies = []
        for distance in range(RING):
            start = (z ^ turned(distance, core)) * (part * CHUNKS) + chunk * part
            target = out.at[pl.ds(pl.multiple_of(start, part), part), :]
            copies.append(pltpu.make_async_copy(ins[distance], target, sems.at[distance]))
        for copy in copies:
            copy.start()
        for copy in copies:
            copy.wait()

    return pl.pallas_call(
        kernel,
        in_specs=[VMEM] * RING + [ANY] * len(earlier) + [SMEM] * len(after),
        out_specs=ANY,
        out_shape=jax.ShapeDtypeStruct((ff, width), bf16),
        scratch_shapes=[pltpu.SemaphoreType.DMA((RING,))],
        input_output_aliases={RING: 0} if earlier else {},
        compiler_params=params(16),
        cost_estimate=BRIEF,
        name="put_rows",
    )(*pieces, *earlier, *after)


def local(acts, out_grads, counts, replica_map, next_map, slot_weights, master, moment1, moment2):
    hidden, grads, weight = acts[0], out_grads[0], slot_weights[0]
    ff = hidden.shape[1]
    scale = ff**-0.5

    first = slot_grads(0, counts, hidden, grads, scale, ())
    second = slot_grads(1, counts, hidden, grads, scale, first[:1])
    along_z = [exchange(move_z, first), exchange(move_z, second)]
    sums = by_expert(replica_map, along_z[0])
    early = exchange(move_y, sums)
    terms, turn = act_terms(counts, grads, weight, scale, (sums[0], along_z[1][1]))
    sums = by_expert(replica_map, along_z[1], (turn,), early[1:])
    late = exchange(move_y, sums)
    *state, rows, turn = adam(0, early, (master, moment1, moment2), (), 1, sums[:1])
    terms, turn = lax.optimization_barrier((terms, turn))
    act_grads = lax.psum_scatter(terms, "shard", scatter_dimension=0, tiled=False)
    fresh = [exchange(move_y, [rows] * RING)]
    *state, rows = adam(1, late, (master, moment1, moment2), tuple(state))
    fresh.append(exchange(move_y, [rows] * RING))
    wanted = [exchange(move_z, by_slot(next_map, pieces)) for pieces in fresh]
    new_weight = put_rows(0, wanted[0], ff, (), (turn,))
    new_weight = put_rows(1, wanted[1], ff, (new_weight,))
    return (new_weight[None], *state, act_grads[None])


def solution(mesh):
    placed = (
        P("slot", None, None),
        P("slot", None, "shard"),
        P("slot"),
        P(),
        P(),
        P("slot", None, "shard"),
        P("slot", "shard"),
        P("slot", "shard"),
        P("slot", "shard"),
    )
    return jax.shard_map(
        local,
        mesh=mesh,
        in_specs=placed,
        out_specs=(
            P("slot", None, "shard"),
            P("slot", "shard"),
            P("slot", "shard"),
            P("slot", "shard"),
            P("slot", None, "shard"),
        ),
        check_vma=False,
    )
```

```python
import functools

import jax
import jax.numpy as jnp
from jax import lax
from jax.experimental import pallas as pl
from jax.experimental.pallas import tpu as pltpu
from jax.sharding import PartitionSpec as P

beta_one = 0.9
beta_two = 0.95
learn_rate = 0.5
weight_decay = 0.1
epsilon = 1e-08
adam_step = 20

RING = 4
CHUNKS = 2
bf16 = jnp.bfloat16
f32 = jnp.float32


def params(limit, *semantics):
    return pltpu.CompilerParams(vmem_limit_bytes=int(limit * 2**20), dimension_semantics=semantics or None)


BUSY = pl.CostEstimate(flops=10_000_000_000, bytes_accessed=14_000_000, transcendentals=0)
BRIEF = pl.CostEstimate(flops=0, bytes_accessed=1024, transcendentals=0)
TURN = jax.ShapeDtypeStruct((1,), jnp.int32)
VMEM = pl.BlockSpec(memory_space=pltpu.VMEM)
SMEM = pl.BlockSpec(memory_space=pltpu.SMEM)
ANY = pl.BlockSpec(memory_space=pl.ANY)
HBM = pl.BlockSpec(memory_space=pltpu.HBM)


def swapped(bits):
    return ((bits & 1) << 1) | (bits >> 1)


def turned(index, core):
    distance = swapped(index)
    return distance ^ ((distance & 1) * 2 * core)


def index_of(distance, core):
    return swapped(distance ^ ((distance & 1) * 2 * core))


def along(stride):
    def move(value, distance):
        pairs = [
            (slot * 2 * RING + shard, (slot ^ (turned(distance, shard % 2) * stride)) * 2 * RING + shard)
            for slot in range(RING * RING)
            for shard in range(2 * RING)
        ]
        return lax.ppermute(value, ("slot", "shard"), pairs)

    return move


move_z = along(1)
move_y = along(RING)


def exchange(move, pieces):
    return [pieces[0]] + [move(pieces[distance], distance) for distance in range(1, RING)]


def my_place():
    slot = lax.axis_index("slot")
    return slot // RING, slot % RING, lax.axis_index("shard") % 2


def slot_grads(chunk, counts, acts, out_grads, scale, after):
    tokens, ff = acts.shape
    width = out_grads.shape[1]
    quarter = ff // RING
    part = quarter // CHUNKS
    blocks = [256, 512, 768, 768, 768]
    starts = [sum(blocks[:i]) for i in range(len(blocks))]
    assert sum(blocks) == tokens

    def kernel(count_ref, acts_hbm, grads_hbm, *rest):
        outs, (acts_ref, grads_ref, total, sems) = rest[-4 - RING : -4], rest[-4:]
        _, z, core = my_place()
        copies = []
        for i, (start, block) in enumerate(zip(starts, blocks)):
            rows = pl.ds(start, block)
            group = [pltpu.make_async_copy(grads_hbm.at[rows, :], grads_ref.at[rows, :], sems.at[i, RING])]
            for distance in range(RING):
                column = pl.multiple_of((z ^ turned(distance, core)) * quarter + chunk * part, part)
                source = acts_hbm.at[rows, pl.ds(column, part)]
                target = acts_ref.at[rows, pl.ds(distance * part, part)]
                group.append(pltpu.make_async_copy(source, target, sems.at[i, distance]))
            copies.append(group)
        for group in copies:
            for copy in group:
                copy.start()
        for i, (start, block) in enumerate(zip(starts, blocks)):
            for copy in copies[i]:
                copy.wait()
            rows = lax.broadcasted_iota(jnp.int32, (block, width), 0)
            grads = grads_ref[start : start + block, :]
            masked = jnp.where(rows < count_ref[0] - start, grads, jnp.zeros_like(grads))
            term = lax.dot_general(
                acts_ref[start : start + block, :], masked, (((0,), (0,)), ((), ())), preferred_element_type=f32
            )
            if i < len(blocks) - 1:
                total[...] = term if i == 0 else total[...] + term
            else:
                term = ((total[...] + term) * scale).astype(bf16)
                for distance in range(RING):
                    outs[distance][...] = term[distance * part : (distance + 1) * part, :]

    return pl.pallas_call(
        kernel,
        in_specs=[SMEM, HBM, HBM] + [ANY] * len(after),
        out_specs=[VMEM] * RING,
        out_shape=[jax.ShapeDtypeStruct((part, width), bf16)] * RING,
        scratch_shapes=[
            pltpu.VMEM((tokens, RING * part), bf16),
            pltpu.VMEM((tokens, width), bf16),
            pltpu.VMEM((RING * part, width), f32),
            pltpu.SemaphoreType.DMA((len(blocks), RING + 1)),
        ],
        compiler_params=params(57.25),
        cost_estimate=BUSY,
        name="slot_grads",
    )(counts, acts, out_grads, *after)


def act_terms(counts, out_grads, weight, scale, after):
    tokens, width = out_grads.shape
    ff = weight.shape[0]
    block = 1024
    steps = tokens // block
    columns = ff // (2 * RING)

    def kernel(count_ref, grads_ref, weight_ref, *rest):
        out_ref, turn_ref = rest[-2:]
        turn_ref[0] = 0
        live = count_ref[0] - pl.program_id(0) * block
        term = lax.dot_general(grads_ref[...], weight_ref[...], (((1,), (1,)), ((), ())), preferred_element_type=f32)
        rows = lax.broadcasted_iota(jnp.int32, term.shape, 0)
        term = jnp.where(rows < live, term * scale, 0.0).astype(bf16)
        for piece in range(2 * RING):
            out_ref[piece] = term[:, piece * columns : (piece + 1) * columns]

    return pl.pallas_call(
        kernel,
        grid_spec=pltpu.PrefetchScalarGridSpec(
            num_scalar_prefetch=1,
            grid=(steps,),
            in_specs=[
                pl.BlockSpec((block, width), lambda i, c: (i, 0)),
                pl.BlockSpec((ff, width), lambda i, c: (0, 0)),
            ]
            + [ANY] * len(after),
            out_specs=[pl.BlockSpec((2 * RING, block, columns), lambda i, c: (0, i, 0)), SMEM],
        ),
        out_shape=[jax.ShapeDtypeStruct((2 * RING, tokens, columns), bf16), TURN],
        compiler_params=params(50, "arbitrary"),
        cost_estimate=BUSY,
        name="act_terms",
    )(counts, out_grads, weight, *after)


def by_expert(replica_map, pieces, after=(), behind=()):
    shape = pieces[0].shape

    def kernel(map_ref, *refs):
        ins, outs = refs[:RING], refs[-RING:]
        y, z, core = my_place()
        values = [ref[...].astype(f32) for ref in ins]
        held = [map_ref[RING * y + (z ^ turned(distance, core))] for distance in range(RING)]
        for step in range(RING):
            expert = y ^ turned(step, core)
            total = jnp.where(held[0] == expert, values[0], 0.0)
            for value, one in zip(values[1:], held[1:]):
                total = total + jnp.where(one == expert, value, 0.0)
            outs[step][...] = total.astype(bf16)

    return pl.pallas_call(
        kernel,
        in_specs=[SMEM] + [VMEM] * RING + [SMEM] * len(after) + [ANY] * len(behind),
        out_specs=[VMEM] * RING,
        out_shape=[jax.ShapeDtypeStruct(shape, bf16)] * RING,
        compiler_params=params(16),
        cost_estimate=BRIEF,
        name="by_expert",
    )(replica_map, *pieces, *after, *behind)


def adam_update(grad_total, master, moment1, moment2):
    new_first = beta_one * moment1 + (1.0 - beta_one) * grad_total
    new_second = beta_two * moment2 + (1.0 - beta_two) * grad_total * grad_total
    first_hat = new_first / (1.0 - beta_one**adam_step)
    second_hat = new_second / (1.0 - beta_two**adam_step)
    update = first_hat / (jnp.sqrt(second_hat) + epsilon)
    master_new = master - learn_rate * (update + weight_decay * master)
    return (master_new, new_first, new_second)


def adam(chunk, pieces, state, earlier, turns=0, behind=()):
    rows, width = state[0].shape
    part = rows // CHUNKS

    def kernel(*refs):
        terms = [ref[...].astype(f32) for ref in refs[:RING]]
        master, moment1, moment2 = refs[RING : RING + 3]
        outs = refs[-4 - turns :]
        if turns:
            outs[4][0] = 0
        grad = (terms[0] + terms[1]) + (terms[2] + terms[3])
        master_new, new_first, new_second = adam_update(grad, master[...], moment1[...], moment2[...])
        outs[0][...] = master_new
        outs[1][...] = new_first
        outs[2][...] = new_second
        outs[3][...] = master_new.astype(bf16)

    whole = jax.ShapeDtypeStruct((rows, width), f32)
    mine = pl.BlockSpec((part, width), lambda i: (chunk, 0))
    return pl.pallas_call(
        kernel,
        grid=(1,),
        in_specs=[pl.BlockSpec((part, width), lambda i: (0, 0))] + [VMEM] * (RING - 1) + [mine] * 3 + [ANY] * (len(earlier) + len(behind)),
        out_specs=[mine] * 3 + [VMEM] + [SMEM] * turns,
        out_shape=[whole] * 3 + [jax.ShapeDtypeStruct((part, width), bf16)] + [TURN] * turns,
        input_output_aliases={RING + 3 + i: i for i in range(len(earlier))},
        compiler_params=params(16, "arbitrary"),
        cost_estimate=BRIEF,
        name="adam",
    )(*pieces, *state, *earlier, *behind)


def by_slot(next_map, pieces):
    def kernel(map_ref, *refs):
        ins, outs = refs[:RING], refs[RING:]
        y, z, core = my_place()
        for distance in range(RING):
            wanted = index_of(map_ref[RING * y + (z ^ turned(distance, core))] ^ y, core)
            for step in range(RING):

                @pl.when(wanted == step)
                def _(step=step, distance=distance):
                    outs[distance][...] = ins[-step][...]

    shape = pieces[0].shape
    return pl.pallas_call(
        kernel,
        in_specs=[SMEM] + [VMEM] * RING,
        out_specs=[VMEM] * RING,
        out_shape=[jax.ShapeDtypeStruct(shape, bf16)] * RING,
        compiler_params=params(16),
        cost_estimate=BRIEF,
        name="by_slot",
    )(next_map, *pieces)


def put_rows(chunk, pieces, ff, earlier, after=()):
    part, width = pieces[0].shape

    def kernel(*refs):
        ins, out, sems = refs[:RING], refs[-2], refs[-1]
        _, z, core = my_place()
        copies = []
        for distance in range(RING):
            start = (z ^ turned(distance, core)) * (part * CHUNKS) + chunk * part
            target = out.at[pl.ds(pl.multiple_of(start, part), part), :]
            copies.append(pltpu.make_async_copy(ins[distance], target, sems.at[distance]))
        for copy in copies:
            copy.start()
        for copy in copies:
            copy.wait()

    return pl.pallas_call(
        kernel,
        in_specs=[VMEM] * RING + [ANY] * len(earlier) + [SMEM] * len(after),
        out_specs=ANY,
        out_shape=jax.ShapeDtypeStruct((ff, width), bf16),
        scratch_shapes=[pltpu.SemaphoreType.DMA((RING,))],
        input_output_aliases={RING: 0} if earlier else {},
        compiler_params=params(16),
        cost_estimate=BRIEF,
        name="put_rows",
    )(*pieces, *earlier, *after)


def local(acts, out_grads, counts, replica_map, next_map, slot_weights, master, moment1, moment2):
    hidden, grads, weight = acts[0], out_grads[0], slot_weights[0]
    ff = hidden.shape[1]
    scale = ff**-0.5

    first = slot_grads(0, counts, hidden, grads, scale, ())
    second = slot_grads(1, counts, hidden, grads, scale, first[:1])
    along_z = [exchange(move_z, first), exchange(move_z, second)]
    sums = by_expert(replica_map, along_z[0])
    early = exchange(move_y, sums)
    terms, turn = act_terms(counts, grads, weight, scale, (sums[0], along_z[1][1]))
    sums = by_expert(replica_map, along_z[1], (turn,), early[1:])
    late = exchange(move_y, sums)
    *state, rows, turn = adam(0, early, (master, moment1, moment2), (), 1, sums[:1])
    terms, turn = lax.optimization_barrier((terms, turn))
    act_grads = lax.psum_scatter(terms, "shard", scatter_dimension=0, tiled=False)
    fresh = [exchange(move_y, [rows] * RING)]
    *state, rows = adam(1, late, (master, moment1, moment2), tuple(state))
    fresh.append(exchange(move_y, [rows] * RING))
    wanted = [exchange(move_z, by_slot(next_map, pieces[:1] + pieces[:0:-1])) for pieces in fresh]
    new_weight = put_rows(0, wanted[0], ff, (), (turn,))
    new_weight = put_rows(1, wanted[1], ff, (new_weight,))
    return (new_weight[None], *state, act_grads[None])


def solution(mesh):
    placed = (
        P("slot", None, None),
        P("slot", None, "shard"),
        P("slot"),
        P(),
        P(),
        P("slot", None, "shard"),
        P("slot", "shard"),
        P("slot", "shard"),
        P("slot", "shard"),
    )
    return jax.shard_map(
        local,
        mesh=mesh,
        in_specs=placed,
        out_specs=(
            P("slot", None, "shard"),
            P("slot", "shard"),
            P("slot", "shard"),
            P("slot", "shard"),
            P("slot", None, "shard"),
        ),
        check_vma=False,
    )
```
